32 devices in a mesh: chan: 8 (over z, core), hour: 4 (over y, x).
Axes of the slice: x: 2, y: 2, z: 4, core: 2. Of those that a mesh axis runs over, the one named last changes fastest.
Arguments:
- spectra: bfloat16 [32, 64, 4096], P('hour', 'chan'), may hold values from -200 to 200
- quality: int32 [64], P('chan'), may hold values 0 or 1
- plan: int32 [4], replicated, may hold values from 1 to 7, as said below
Outputs:
- correlations: float32 [4, 8, 64, 512], P(None, 'hour', 'chan')
The draws below stay inside these ranges and needn't reach their ends.
Inputs may be any that keep to these rules, and one draw needn't show every extreme that they name: `plan`: distinct numbers; 1 and 7 are among them.
All inputs are finite; a program needn't handle non-finite values. No bound on the sum of `quality` on one device may be relied on, other than what follows from the above.
Results may differ from the reference program's by a relative error of at most 0.004.
Values may be sent and summed in bfloat16 or wider, within the bound.
A program may use at most 320 MiB of HBM per device.

```python
import math
import jax
import jax.numpy as jnp
from jax import lax

FREQS = 2048
BAND = 64
LAGS = 512
ROUNDS = 4
C_DEV = 8
CHANNELS = 64
HOURS = 32
N_CHAN = 8


def draw_spectra(key, part):
    keys = jax.random.split(key, 3)
    shape = (HOURS, CHANNELS, 2 * FREQS)
    base = jnp.clip(jax.random.normal(keys[0], shape, jnp.float32), -6.0, 6.0)
    row_scale = jnp.exp(jax.random.uniform(keys[1], (HOURS, CHANNELS, 1), jnp.float32) * math.log(10.0))
    col_half = jnp.exp(jax.random.uniform(keys[2], (1, 1, FREQS), jnp.float32) * math.log(10.0))
    col_scale = jnp.concatenate([col_half, col_half], axis=-1)
    return (base * row_scale * col_scale * 0.3).astype(jnp.bfloat16)


def draw_plan(key, part):
    others = jax.random.permutation(key, N_CHAN - 3)[:ROUNDS - 2].astype(jnp.int32) + 2
    values = jnp.concatenate([jnp.array([N_CHAN - 1, 1], dtype=jnp.int32), others])
    order = jax.random.permutation(jax.random.fold_in(key, 7), ROUNDS)
    return values[order]


def touch_ends(entries, own_key, smallest, top_value):
    longest = entries.shape.index(max(entries.shape))
    spots = []
    for shift in (0, 1):
        where = [jax.random.randint(jax.random.fold_in(own_key, axis), (), 0, length) for axis, length in enumerate(entries.shape)]
        where[longest] = (where[longest] + shift) % entries.shape[longest]
        spots.append(tuple(where))
    return entries.at[spots[0]].set(smallest).at[spots[1]].set(top_value)


def setup_inputs(seed: int = 0) -> dict:
    splits = jax.random.split(jax.random.key(seed), 4)
    return {
        "spectra": draw_spectra(jax.random.fold_in(splits[3], 71), 0),
        "quality": touch_ends((jax.random.randint(splits[1], (CHANNELS,), 0, 4) < 3).astype(jnp.int32), jax.random.fold_in(splits[1], 1), 0, 1),
        "plan": draw_plan(jax.random.fold_in(splits[3], 71), 0),
    }


def whiten(spectra, quality):
    hours, chans, width = spectra.shape
    n_freq = width // 2
    values = spectra.astype(jnp.float32)
    real_part = values[..., :n_freq]
    imag_part = values[..., n_freq:]
    power_sum = real_part * real_part + imag_part * imag_part
    band_mean = lax.optimization_barrier(jnp.mean(power_sum.reshape(hours, chans, n_freq // BAND, BAND), axis=-1, keepdims=True))
    gain_band = lax.rsqrt(band_mean + 1e-06)
    gain_full = jnp.broadcast_to(gain_band, (hours, chans, n_freq // BAND, BAND)).reshape(hours, chans, n_freq)
    gain_both = jnp.concatenate([gain_full, gain_full], axis=-1)
    scaled = values * gain_both * quality.astype(jnp.float32)[None, :, None]
    return scaled.astype(jnp.bfloat16)

def lag_table(n_freq, total_hours):
    freq_index = jnp.arange(n_freq, dtype=jnp.int32)[:, None]
    lag_index = jnp.arange(LAGS, dtype=jnp.int32)[None, :] - LAGS // 2
    phase_int = freq_index * lag_index % (2 * n_freq)
    angle = jnp.pi * phase_int.astype(jnp.float32) / n_freq
    factor = 1.0 / jnp.sqrt(jnp.float32(total_hours * n_freq))
    return jnp.concatenate([jnp.cos(angle), -jnp.sin(angle)], axis=0) * factor

def reference(spectra, quality, plan):
    whitened = whiten(spectra, quality).astype(jnp.float32)
    n_freq = FREQS
    blocks = whitened.reshape(HOURS, N_CHAN, C_DEV, 2 * n_freq)
    own_re = blocks[..., :n_freq]
    own_im = blocks[..., n_freq:]
    weights = lag_table(n_freq, HOURS)
    hp = lax.Precision.HIGHEST
    results = []
    for rnd_index in range(ROUNDS):
        partners = jnp.bitwise_xor(jnp.arange(N_CHAN, dtype=jnp.int32), plan[rnd_index])
        partner = jnp.take(blocks, partners, axis=1)
        far_re = partner[..., :n_freq]
        far_im = partner[..., n_freq:]
        cross_re = jnp.einsum('hbjf,hbif->bjif', far_re, own_re, precision=hp) + jnp.einsum('hbjf,hbif->bjif', far_im, own_im, precision=hp)
        cross_im = jnp.einsum('hbjf,hbif->bjif', far_re, own_im, precision=hp) - jnp.einsum('hbjf,hbif->bjif', far_im, own_re, precision=hp)
        cross_spec = jnp.concatenate([cross_re, cross_im], axis=-1)
        flat = cross_spec.reshape(N_CHAN * C_DEV * C_DEV, 2 * n_freq)
        lagged = jnp.dot(flat, weights, precision=hp, preferred_element_type=jnp.float32)
        lagged = lagged.reshape(N_CHAN, C_DEV, C_DEV, LAGS).transpose(1, 0, 2, 3).reshape(C_DEV, N_CHAN * C_DEV, LAGS)
        results.append(lagged)
    return jnp.stack(results)
```

```python
import functools

import jax
import jax.numpy as jnp
import ml_dtypes
import numpy as np
from jax import lax
from jax.experimental import pallas as pl
from jax.experimental.pallas import tpu as pltpu
from jax.sharding import PartitionSpec as P

BAND = 64
LAGS = 512
ROUNDS = 4
CHUNKS = 4
LANES = 128
MESH = pl.DeviceIdType.MESH
F32 = jnp.float32
BF16 = jnp.bfloat16


def lag_tables(n_freq, total_hours, chunks):
    lag = np.arange(LAGS, dtype=np.int64)[None, :] - LAGS // 2
    phase = np.arange(n_freq, dtype=np.int64)[:, None] * lag % (2 * n_freq)
    angle = np.pi * phase.astype(np.float64) / n_freq
    factor = 1.0 / np.sqrt(float(total_hours * n_freq))
    part = n_freq // chunks
    cos = (np.cos(angle) * factor).reshape(chunks, part, LAGS)
    sin = (-np.sin(angle) * factor).reshape(chunks, part, LAGS)
    table = np.concatenate([cos, sin], axis=1)
    high = table.astype(ml_dtypes.bfloat16)
    low = (table - high.astype(np.float64)).astype(ml_dtypes.bfloat16)
    return high, low


def split(value):
    high = value.astype(BF16)
    return high, (value - high.astype(F32)).astype(BF16)


def kernel(dims, plan_ref, spectra_ref, quality_ref, high_ref, low_ref, out_ref, *scratch):
    n_chan, n_hour, hours, chans, n_freq = dims
    held = scratch[:CHUNKS]
    (own, far, cross, total, arrived, high, low, table_sem,
     line_send, line_recv, twin_send, twin_recv, sum_send, sum_recv) = scratch[CHUNKS:]
    n_chip = n_chan // 2
    rows = hours * chans
    part = n_freq // CHUNKS
    per_hour = chans // n_hour
    share = ROUNDS * per_hour * chans
    me, my_hour = lax.axis_index("chan"), lax.axis_index("hour")
    chip, core = me // 2, me % 2
    twin = chip * 2 + 1 - core
    has = (chip < n_chip - 1, chip > 0)
    neighbour = (jnp.minimum(chip + 1, n_chip - 1) * 2 + core, jnp.maximum(chip - 1, 0) * 2 + core)

    loads = [pltpu.make_async_copy(high_ref, high, table_sem.at[0]),
             pltpu.make_async_copy(low_ref, low, table_sem.at[1])]
    for load in loads:
        load.start()

    barrier = pltpu.get_barrier_semaphore()
    pl.semaphore_signal(barrier, inc=1, device_id=(twin, my_hour), device_id_type=MESH)
    for way in range(2):
        @pl.when(has[way])
        def _(way=way):
            pl.semaphore_signal(barrier, inc=1, device_id=(neighbour[way], my_hour), device_id_type=MESH)
    for step in range(1, n_hour):
        pl.semaphore_signal(barrier, inc=1, device_id=(me, lax.rem(my_hour + step, n_hour)), device_id_type=MESH)

    half = lax.broadcasted_iota(jnp.int32, (LANES, LANES), 0) // BAND
    half_out = lax.broadcasted_iota(jnp.int32, (LANES, LANES), 1) // BAND
    ones = jnp.where(half == half_out, 1.0, 0.0).astype(BF16)
    quality = quality_ref[...]

    def whiten(chunk):
        def tile(at, carry):
            cols = pl.multiple_of(at * LANES, LANES)
            re_at = pl.multiple_of(chunk * part + cols, LANES)
            im_at = pl.multiple_of(n_freq + chunk * part + cols, LANES)
            re = spectra_ref[:, :, pl.ds(re_at, LANES)].astype(F32).reshape(rows, LANES)
            im = spectra_ref[:, :, pl.ds(im_at, LANES)].astype(F32).reshape(rows, LANES)
            power = re * re + im * im
            first, rest = power.astype(BF16), power
            rest = rest - first.astype(F32)
            second = rest.astype(BF16)
            third = (rest - second.astype(F32)).astype(BF16)
            band = jnp.dot(first, ones, preferred_element_type=F32)
            band += jnp.dot(second, ones, preferred_element_type=F32)
            band += jnp.dot(third, ones, preferred_element_type=F32)
            gain = lax.rsqrt(band * (1.0 / BAND) + 1e-6)
            re_out = (re * gain * quality).astype(BF16)
            im_out = (im * gain * quality).astype(BF16)
            im_cols = pl.multiple_of(part + cols, LANES)
            held[chunk][me, :, pl.ds(cols, LANES)] = re_out
            held[chunk][me, :, pl.ds(im_cols, LANES)] = im_out
            own[chunk, :, pl.ds(cols, LANES)] = re_out.astype(F32)
            own[chunk, :, pl.ds(im_cols, LANES)] = im_out.astype(F32)
            return carry

        lax.fori_loop(0, part // LANES, tile, 0)

    def line(chunk, step, way, block):
        slot = held[chunk].at[block * 2 + core]
        return pltpu.make_async_remote_copy(
            src_ref=slot, dst_ref=slot,
            send_sem=line_send.at[chunk, step, way], recv_sem=line_recv.at[chunk, step, way],
            device_id=(neighbour[way], my_hour), device_id_type=MESH)

    def to_twin(chunk, step, way, block, side):
        slot = held[chunk].at[block * 2 + side]
        return pltpu.make_async_remote_copy(
            src_ref=slot, dst_ref=slot,
            send_sem=twin_send.at[chunk, step, way], recv_sem=twin_recv.at[chunk, step, way],
            device_id=(twin, my_hour), device_id_type=MESH)

    def sends(step, way):
        block = chip - step if way == 0 else chip + step
        ok = block >= 0 if way == 0 else block <= n_chip - 1
        return jnp.clip(block, 0, n_chip - 1), jnp.logical_and(ok, has[way])

    def receives(step, way):
        block = chip - 1 - step if way == 0 else chip + 1 + step
        ok = block >= 0 if way == 0 else block <= n_chip - 1
        return jnp.clip(block, 0, n_chip - 1), ok

    def start_line(chunk, step, way):
        block, ok = sends(step, way)
        pl.when(ok)(lambda: line(chunk, step, way, block).start())

    whiten(0)
    pl.semaphore_wait(barrier, n_hour + (chip < n_chip - 1).astype(jnp.int32) + (chip > 0).astype(jnp.int32))

    for chunk in range(CHUNKS):
        if chunk:
            whiten(chunk)
        for way in range(2):
            start_line(chunk, 0, way)
        to_twin(chunk, 0, 0, chip, core).start()

    def pass_on(chunk, step):
        for way in range(2):
            block, ok = receives(step, way)

            @pl.when(ok)
            def _(way=way, block=block):
                line(chunk, step, way, block).wait_recv()
                if step + 1 < n_chip - 1:
                    start_line(chunk, step + 1, way)
                to_twin(chunk, step + 1, way, block, core).start()

    def work(chunk):
        to_twin(chunk, 0, 0, chip, 1 - core).wait_recv()
        for step in range(n_chip - 1):
            for way in range(2):
                block, ok = receives(step, way)
                pl.when(ok)(lambda: to_twin(chunk, step + 1, way, block, 1 - core).wait_recv())
        if chunk == 0:
            for load in loads:
                load.wait()
        for rnd in range(ROUNDS):
            partner = jnp.bitwise_xor(me, plan_ref[rnd])
            far[rnd] = held[chunk][partner].astype(F32)

        def tile(at, carry):
            rnd, cols = at // (part // LANES), at % (part // LANES) * LANES
            re_at = pl.ds(pl.multiple_of(cols, LANES), LANES)
            im_at = pl.ds(pl.multiple_of(part + cols, LANES), LANES)
            sums_re = [jnp.zeros((chans, LANES), F32)] * chans
            sums_im = [jnp.zeros((chans, LANES), F32)] * chans
            for hour in range(hours):
                own_re = own[chunk, hour * chans:(hour + 1) * chans, re_at]
                own_im = own[chunk, hour * chans:(hour + 1) * chans, im_at]
                for j in range(chans):
                    far_re = far[rnd, hour * chans + j:hour * chans + j + 1, re_at]
                    far_im = far[rnd, hour * chans + j:hour * chans + j + 1, im_at]
                    sums_re[j] += own_re * far_re + own_im * far_im
                    sums_im[j] += own_im * far_re - own_re * far_im
            for j in range(chans):
                start = (j // per_hour) * share + (rnd * per_hour + j % per_hour) * chans
                at_rows = pl.ds(pl.multiple_of(start, 8), chans)
                cross[at_rows, re_at] = sums_re[j]
                cross[at_rows, im_at] = sums_im[j]
            return carry

        lax.fori_loop(0, ROUNDS * (part // LANES), tile, 0)

        first, second = split(cross[...])
        lagged = jnp.dot(first, high[chunk], preferred_element_type=F32)
        lagged += jnp.dot(second, high[chunk], preferred_element_type=F32)
        lagged += jnp.dot(first, low[chunk], preferred_element_type=F32)
        if chunk == 0:
            total[...] = lagged
        else:
            total[...] += lagged

    for step in range(n_chip - 2):
        for chunk in range(CHUNKS):
            pass_on(chunk, step)
    for chunk in range(CHUNKS):
        pass_on(chunk, n_chip - 2)
        if chunk:
            work(chunk - 1)
    work(CHUNKS - 1)

    def give(step):
        goal = lax.rem(my_hour + step, n_hour)
        return pltpu.make_async_remote_copy(
            src_ref=total.at[pl.ds(pl.multiple_of(goal * share, 8), share)],
            dst_ref=arrived.at[step - 1],
            send_sem=sum_send.at[step - 1], recv_sem=sum_recv.at[step - 1],
            device_id=(me, goal), device_id_type=MESH)

    for step in range(1, n_hour):
        give(step).start()

    for chunk in range(CHUNKS):
        to_twin(chunk, 0, 0, chip, core).wait_send()
        for step in range(n_chip - 1):
            for way in range(2):
                block, ok = sends(step, way)
                pl.when(ok)(lambda: line(chunk, step, way, block).wait_send())
                block, ok = receives(step, way)
                pl.when(ok)(lambda: to_twin(chunk, step + 1, way, block, core).wait_send())

    result = total[pl.ds(pl.multiple_of(my_hour * share, 8), share), :]
    for step in range(1, n_hour):
        give(step).wait_recv()
        result += arrived[step - 1]
    out_ref[...] = result.reshape(ROUNDS, per_hour, chans, LAGS)
    for step in range(1, n_hour):
        give(step).wait_send()


def per_device(spectra, quality, plan):
    hours, chans, width = spectra.shape
    n_freq = width // 2
    n_chan, n_hour = lax.axis_size("chan"), lax.axis_size("hour")
    n_chip = n_chan // 2
    rows = hours * chans
    part = n_freq // CHUNKS
    per_hour = chans // n_hour
    share = ROUNDS * per_hour * chans
    high, low = lag_tables(n_freq, hours * n_hour, CHUNKS)
    by_row = jnp.broadcast_to(
        jnp.tile(quality.astype(F32), hours)[:, None], (rows, LANES))
    vmem = pl.BlockSpec(memory_space=pltpu.VMEM)
    dma = pltpu.SemaphoreType.DMA
    return pl.pallas_call(
        functools.partial(kernel, (n_chan, n_hour, hours, chans, n_freq)),
        out_shape=jax.ShapeDtypeStruct((ROUNDS, per_hour, chans, LAGS), F32),
        in_specs=[pl.BlockSpec(memory_space=pltpu.SMEM), vmem, vmem,
                  pl.BlockSpec(memory_space=pl.ANY), pl.BlockSpec(memory_space=pl.ANY)],
        out_specs=vmem,
        scratch_shapes=[pltpu.VMEM((n_chan, rows, 2 * part), BF16)] * CHUNKS + [
            pltpu.VMEM((CHUNKS, rows, 2 * part), F32),
            pltpu.VMEM((ROUNDS, rows, 2 * part), F32),
            pltpu.VMEM((n_hour * share, 2 * part), F32),
            pltpu.VMEM((n_hour * share, LAGS), F32),
            pltpu.VMEM((n_hour - 1, share, LAGS), F32),
            pltpu.VMEM(high.shape, BF16),
            pltpu.VMEM(low.shape, BF16),
            dma((2,)),
            dma((CHUNKS, n_chip - 1, 2)),
            dma((CHUNKS, n_chip - 1, 2)),
            dma((CHUNKS, n_chip, 2)),
            dma((CHUNKS, n_chip, 2)),
            dma((n_hour - 1,)),
            dma((n_hour - 1,)),
        ],
        compiler_params=pltpu.CompilerParams(
            collective_id=0, has_side_effects=True, vmem_limit_bytes=48 * 1024 * 1024),
    )(plan, spectra, by_row, jnp.asarray(high), jnp.asarray(low))


def solution(mesh):
    return jax.shard_map(
        per_device,
        mesh=mesh,
        in_specs=(P("hour", "chan", None), P("chan"), P()),
        out_specs=P(None, "hour", "chan", None),
        check_vma=False,
    )
```

```python
import functools

import jax
import jax.numpy as jnp
import ml_dtypes
import numpy as np
from jax import lax
from jax.experimental import pallas as pl
from jax.experimental.pallas import tpu as pltpu
from jax.sharding import PartitionSpec as P

BAND = 64
LAGS = 512
ROUNDS = 4
CHUNKS = 8
LANES = 128
MESH = pl.DeviceIdType.MESH
F32 = jnp.float32
BF16 = jnp.bfloat16


def lag_tables(n_freq, total_hours, chunks):
    lag = np.arange(LAGS, dtype=np.int64)[None, :] - LAGS // 2
    phase = np.arange(n_freq, dtype=np.int64)[:, None] * lag % (2 * n_freq)
    angle = np.pi * phase.astype(np.float64) / n_freq
    factor = 1.0 / np.sqrt(float(total_hours * n_freq))
    part = n_freq // chunks
    cos = (np.cos(angle) * factor).reshape(chunks, part, LAGS)
    sin = (-np.sin(angle) * factor).reshape(chunks, part, LAGS)
    table = np.concatenate([cos, sin], axis=1)
    high = table.astype(ml_dtypes.bfloat16)
    low = (table - high.astype(np.float64)).astype(ml_dtypes.bfloat16)
    return high, low


def split(value):
    high = value.astype(BF16)
    return high, (value - high.astype(F32)).astype(BF16)


def kernel(dims, plan_ref, spectra_hbm, quality_ref, high_ref, low_ref, out_ref, *scratch):
    n_chan, n_hour, hours, chans, n_freq = dims
    held = scratch[:CHUNKS]
    (own, far, cross, total, arrived, rounded, raw, high, low, table_sem,
     line_send, line_recv, twin_send, twin_recv, sum_send, sum_recv) = scratch[CHUNKS:]
    n_chip = n_chan // 2
    rows = hours * chans
    part = n_freq // CHUNKS
    per_hour = chans // n_hour
    share = ROUNDS * per_hour * chans
    me, my_hour = lax.axis_index("chan"), lax.axis_index("hour")
    chip, core = me // 2, me % 2
    twin = chip * 2 + 1 - core
    has = (chip < n_chip - 1, chip > 0)
    neighbour = (jnp.minimum(chip + 1, n_chip - 1) * 2 + core, jnp.maximum(chip - 1, 0) * 2 + core)

    fetch = pltpu.make_async_copy(spectra_hbm, raw, table_sem.at[2])
    fetch.start()
    loads = [pltpu.make_async_copy(high_ref, high, table_sem.at[0]),
             pltpu.make_async_copy(low_ref, low, table_sem.at[1])]
    for load in loads:
        load.start()

    barrier = pltpu.get_barrier_semaphore()
    pl.semaphore_signal(barrier, inc=1, device_id=(twin, my_hour), device_id_type=MESH)
    for way in range(2):
        @pl.when(has[way])
        def _(way=way):
            pl.semaphore_signal(barrier, inc=1, device_id=(neighbour[way], my_hour), device_id_type=MESH)
    for step in range(1, n_hour):
        pl.semaphore_signal(barrier, inc=1, device_id=(me, lax.rem(my_hour + step, n_hour)), device_id_type=MESH)

    half = lax.broadcasted_iota(jnp.int32, (LANES, LANES), 0) // BAND
    half_out = lax.broadcasted_iota(jnp.int32, (LANES, LANES), 1) // BAND
    ones = jnp.where(half == half_out, 1.0, 0.0).astype(BF16)
    channel = lax.broadcasted_iota(jnp.int32, (chans, LANES), 0)
    quality = jnp.zeros((chans, LANES), F32)
    for c in range(chans):
        quality = jnp.where(channel == c, quality_ref[c].astype(F32), quality)
    quality = jnp.broadcast_to(quality[None], (hours, chans, LANES)).reshape(rows, LANES)

    def whiten(chunk):
        def tile(at, carry):
            cols = pl.multiple_of(at * LANES, LANES)
            re_at = pl.multiple_of(chunk * part + cols, LANES)
            im_at = pl.multiple_of(n_freq + chunk * part + cols, LANES)
            re = raw[:, :, pl.ds(re_at, LANES)].astype(F32).reshape(rows, LANES)
            im = raw[:, :, pl.ds(im_at, LANES)].astype(F32).reshape(rows, LANES)
            power = re * re + im * im
            first, rest = power.astype(BF16), power
            rest = rest - first.astype(F32)
            second = rest.astype(BF16)
            third = (rest - second.astype(F32)).astype(BF16)
            band = jnp.dot(first, ones, preferred_element_type=F32)
            band += jnp.dot(second, ones, preferred_element_type=F32)
            band += jnp.dot(third, ones, preferred_element_type=F32)
            gain = lax.rsqrt(band * (1.0 / BAND) + 1e-6)
            re_out = (re * gain * quality).astype(BF16)
            im_out = (im * gain * quality).astype(BF16)
            im_cols = pl.multiple_of(part + cols, LANES)
            held[chunk][me, :, pl.ds(cols, LANES)] = re_out
            held[chunk][me, :, pl.ds(im_cols, LANES)] = im_out
            own[chunk, :, pl.ds(cols, LANES)] = re_out.astype(F32)
            own[chunk, :, pl.ds(im_cols, LANES)] = im_out.astype(F32)
            return carry

        lax.fori_loop(0, part // LANES, tile, 0)

    def line(chunk, step, way, block):
        slot = held[chunk].at[block * 2 + core]
        return pltpu.make_async_remote_copy(
            src_ref=slot, dst_ref=slot,
            send_sem=line_send.at[chunk, step, way], recv_sem=line_recv.at[chunk, step, way],
            device_id=(neighbour[way], my_hour), device_id_type=MESH)

    def to_twin(chunk, step, way, block, side):
        slot = held[chunk].at[block * 2 + side]
        return pltpu.make_async_remote_copy(
            src_ref=slot, dst_ref=slot,
            send_sem=twin_send.at[chunk, step, way], recv_sem=twin_recv.at[chunk, step, way],
            device_id=(twin, my_hour), device_id_type=MESH)

    def sends(step, way):
        block = chip - step if way == 0 else chip + step
        ok = block >= 0 if way == 0 else block <= n_chip - 1
        return jnp.clip(block, 0, n_chip - 1), jnp.logical_and(ok, has[way])

    def receives(step, way):
        block = chip - 1 - step if way == 0 else chip + 1 + step
        ok = block >= 0 if way == 0 else block <= n_chip - 1
        return jnp.clip(block, 0, n_chip - 1), ok

    def start_line(chunk, step, way):
        block, ok = sends(step, way)
        pl.when(ok)(lambda: line(chunk, step, way, block).start())

    fetch.wait()
    whiten(0)
    pl.semaphore_wait(barrier, n_hour + (chip < n_chip - 1).astype(jnp.int32) + (chip > 0).astype(jnp.int32))

    for chunk in range(CHUNKS):
        if chunk:
            whiten(chunk)
        for way in range(2):
            start_line(chunk, 0, way)
        to_twin(chunk, 0, 0, chip, core).start()

    def pass_on(chunk, step):
        for way in range(2):
            block, ok = receives(step, way)

            @pl.when(ok)
            def _(way=way, block=block):
                line(chunk, step, way, block).wait_recv()
                if step + 1 < n_chip - 1:
                    start_line(chunk, step + 1, way)
                to_twin(chunk, step + 1, way, block, core).start()

    def work(chunk):
        to_twin(chunk, 0, 0, chip, 1 - core).wait_recv()
        for step in range(n_chip - 1):
            for way in range(2):
                block, ok = receives(step, way)
                pl.when(ok)(lambda: to_twin(chunk, step + 1, way, block, 1 - core).wait_recv())
        if chunk == 0:
            for load in loads:
                load.wait()
        for rnd in range(ROUNDS):
            partner = jnp.bitwise_xor(me, plan_ref[rnd])
            far[rnd] = held[chunk][partner].astype(F32)

        def tile(at, carry):
            rnd, cols = at // (part // LANES), at % (part // LANES) * LANES
            re_at = pl.ds(pl.multiple_of(cols, LANES), LANES)
            im_at = pl.ds(pl.multiple_of(part + cols, LANES), LANES)
            sums_re = [jnp.zeros((chans, LANES), F32)] * chans
            sums_im = [jnp.zeros((chans, LANES), F32)] * chans
            for hour in range(hours):
                own_re = own[chunk, hour * chans:(hour + 1) * chans, re_at]
                own_im = own[chunk, hour * chans:(hour + 1) * chans, im_at]
                for j in range(chans):
                    far_re = far[rnd, hour * chans + j:hour * chans + j + 1, re_at]
                    far_im = far[rnd, hour * chans + j:hour * chans + j + 1, im_at]
                    sums_re[j] += own_re * far_re + own_im * far_im
                    sums_im[j] += own_im * far_re - own_re * far_im
            for j in range(chans):
                start = (j // per_hour) * share + (rnd * per_hour + j % per_hour) * chans
                at_rows = pl.ds(pl.multiple_of(start, 8), chans)
                cross[at_rows, re_at] = sums_re[j]
                cross[at_rows, im_at] = sums_im[j]
            return carry

        lax.fori_loop(0, ROUNDS * (part // LANES), tile, 0)

        first, second = split(cross[...])
        lagged = jnp.dot(first, high[chunk], preferred_element_type=F32)
        lagged += jnp.dot(second, high[chunk], preferred_element_type=F32)
        lagged += jnp.dot(first, low[chunk], preferred_element_type=F32)
        if chunk == 0:
            total[...] = lagged
        else:
            total[...] += lagged

    for step in range(n_chip - 2):
        for chunk in range(CHUNKS):
            pass_on(chunk, step)
    for chunk in range(CHUNKS):
        pass_on(chunk, n_chip - 2)
        if chunk:
            work(chunk - 1)
    work(CHUNKS - 1)

    def give(step):
        goal = lax.rem(my_hour + step, n_hour)
        return pltpu.make_async_remote_copy(
            src_ref=rounded.at[pl.ds(pl.multiple_of(goal * share, 8), share)],
            dst_ref=arrived.at[step - 1],
            send_sem=sum_send.at[step - 1], recv_sem=sum_recv.at[step - 1],
            device_id=(me, goal), device_id_type=MESH)

    rounded[...] = total[...].astype(BF16)
    for step in range(1, n_hour):
        give(step).start()

    for chunk in range(CHUNKS):
        to_twin(chunk, 0, 0, chip, core).wait_send()
        for step in range(n_chip - 1):
            for way in range(2):
                block, ok = sends(step, way)
                pl.when(ok)(lambda: line(chunk, step, way, block).wait_send())
                block, ok = receives(step, way)
                pl.when(ok)(lambda: to_twin(chunk, step + 1, way, block, core).wait_send())

    result = total[pl.ds(pl.multiple_of(my_hour * share, 8), share), :]
    for step in range(1, n_hour):
        give(step).wait_recv()
        result += arrived[step - 1].astype(F32)
    out_ref[...] = result.reshape(ROUNDS, per_hour, chans, LAGS)
    for step in range(1, n_hour):
        give(step).wait_send()


def per_device(spectra, quality, plan):
    hours, chans, width = spectra.shape
    n_freq = width // 2
    n_chan, n_hour = lax.axis_size("chan"), lax.axis_size("hour")
    n_chip = n_chan // 2
    rows = hours * chans
    part = n_freq // CHUNKS
    per_hour = chans // n_hour
    share = ROUNDS * per_hour * chans
    high, low = lag_tables(n_freq, hours * n_hour, CHUNKS)
    smem, vmem, hbm = (pl.BlockSpec(memory_space=m) for m in (pltpu.SMEM, pltpu.VMEM, pltpu.HBM))
    dma = pltpu.SemaphoreType.DMA
    return pl.pallas_call(
        functools.partial(kernel, (n_chan, n_hour, hours, chans, n_freq)),
        out_shape=jax.ShapeDtypeStruct((ROUNDS, per_hour, chans, LAGS), F32),
        in_specs=[smem, hbm, smem, hbm, hbm],
        out_specs=vmem,
        scratch_shapes=[pltpu.VMEM((n_chan, rows, 2 * part), BF16)] * CHUNKS + [
            pltpu.VMEM((CHUNKS, rows, 2 * part), F32),
            pltpu.VMEM((ROUNDS, rows, 2 * part), F32),
            pltpu.VMEM((n_hour * share, 2 * part), F32),
            pltpu.VMEM((n_hour * share, LAGS), F32),
            pltpu.VMEM((n_hour - 1, share, LAGS), BF16),
            pltpu.VMEM((n_hour * share, LAGS), BF16),
            pltpu.VMEM(spectra.shape, BF16),
            pltpu.VMEM(high.shape, BF16),
            pltpu.VMEM(low.shape, BF16),
            dma((3,)),
            dma((CHUNKS, n_chip - 1, 2)),
            dma((CHUNKS, n_chip - 1, 2)),
            dma((CHUNKS, n_chip, 2)),
            dma((CHUNKS, n_chip, 2)),
            dma((n_hour - 1,)),
            dma((n_hour - 1,)),
        ],
        compiler_params=pltpu.CompilerParams(
            collective_id=0, has_side_effects=True, vmem_limit_bytes=63 * 1024 * 1024 + 960 * 1024),
    )(plan, spectra, quality, jnp.asarray(high), jnp.asarray(low))


def solution(mesh):
    return jax.shard_map(
        per_device,
        mesh=mesh,
        in_specs=(P("hour", "chan", None), P("chan"), P()),
        out_specs=P(None, "hour", "chan", None),
        check_vma=False,
    )
```

```python
import functools

import jax
import jax.numpy as jnp
import ml_dtypes
import numpy as np
from jax import lax
from jax.experimental import pallas as pl
from jax.experimental.pallas import tpu as pltpu
from jax.sharding import PartitionSpec as P

BAND = 64
LAGS = 512
ROUNDS = 4
CHUNKS = 8
LANES = 128
MESH = pl.DeviceIdType.MESH
F32 = jnp.float32
BF16 = jnp.bfloat16


def lag_tables(n_freq, total_hours, chunks):
    lag = np.arange(LAGS, dtype=np.int64)[None, :] - LAGS // 2
    phase = np.arange(n_freq, dtype=np.int64)[:, None] * lag % (2 * n_freq)
    angle = np.pi * phase.astype(np.float64) / n_freq
    factor = 1.0 / np.sqrt(float(total_hours * n_freq))
    part = n_freq // chunks
    cos = (np.cos(angle) * factor).reshape(chunks, part, LAGS)
    sin = (-np.sin(angle) * factor).reshape(chunks, part, LAGS)
    table = np.concatenate([cos, sin], axis=1)
    high = table.astype(ml_dtypes.bfloat16)
    low = (table - high.astype(np.float64)).astype(ml_dtypes.bfloat16)
    return high, low


def split(value):
    high = value.astype(BF16)
    return high, (value - high.astype(F32)).astype(BF16)


def kernel(dims, apart, plan_ref, spectra_hbm, quality_ref, high_ref, low_ref, out_ref, *scratch):
    n_chan, n_hour, hours, chans, n_freq = dims
    held = scratch[:CHUNKS]
    (own, far, cross, total, arrived, rounded, raw, high, low, table_sem,
     line_send, line_recv, twin_send, twin_recv, sum_send, sum_recv) = scratch[CHUNKS:]
    n_chip = n_chan // 2
    rows = hours * chans
    part = n_freq // CHUNKS
    per_hour = chans // n_hour
    share = ROUNDS * per_hour * chans
    me, my_hour = lax.axis_index("chan"), lax.axis_index("hour")
    chip, core = me // 2, me % 2
    twin = chip * 2 + 1 - core
    has = (chip < n_chip - 1, chip > 0)
    neighbour = (jnp.minimum(chip + 1, n_chip - 1) * 2 + core, jnp.maximum(chip - 1, 0) * 2 + core)

    fetch = pltpu.make_async_copy(spectra_hbm, raw, table_sem.at[2])
    fetch.start()
    loads = [pltpu.make_async_copy(high_ref, high, table_sem.at[0]),
             pltpu.make_async_copy(low_ref, low, table_sem.at[1])]
    for load in loads:
        load.start()

    barrier = pltpu.get_barrier_semaphore()
    pl.semaphore_signal(barrier, inc=1, device_id=(twin, my_hour), device_id_type=MESH)
    for way in range(2):
        @pl.when(has[way])
        def _(way=way):
            pl.semaphore_signal(barrier, inc=1, device_id=(neighbour[way], my_hour), device_id_type=MESH)
    for step in range(1, n_hour):
        pl.semaphore_signal(barrier, inc=1, device_id=(me, lax.rem(my_hour + step, n_hour)), device_id_type=MESH)

    half = lax.broadcasted_iota(jnp.int32, (LANES, LANES), 0) // BAND
    half_out = lax.broadcasted_iota(jnp.int32, (LANES, LANES), 1) // BAND
    ones = jnp.where(half == half_out, 1.0, 0.0).astype(BF16)
    channel = lax.broadcasted_iota(jnp.int32, (chans, LANES), 0)
    quality = jnp.zeros((chans, LANES), F32)
    for c in range(chans):
        quality = jnp.where(channel == c, quality_ref[c].astype(F32), quality)
    quality = jnp.broadcast_to(quality[None], (hours, chans, LANES)).reshape(rows, LANES)

    def whiten(chunk):
        def tile(at, carry):
            cols = pl.multiple_of(at * LANES, LANES)
            re_at = pl.multiple_of(chunk * part + cols, LANES)
            im_at = pl.multiple_of(n_freq + chunk * part + cols, LANES)
            re = raw[:, :, pl.ds(re_at, LANES)].astype(F32).reshape(rows, LANES)
            im = raw[:, :, pl.ds(im_at, LANES)].astype(F32).reshape(rows, LANES)
            power = re * re + im * im
            first, rest = power.astype(BF16), power
            rest = rest - first.astype(F32)
            second = rest.astype(BF16)
            third = (rest - second.astype(F32)).astype(BF16)
            band = jnp.dot(first, ones, preferred_element_type=F32)
            band += jnp.dot(second, ones, preferred_element_type=F32)
            band += jnp.dot(third, ones, preferred_element_type=F32)
            gain = lax.rsqrt(band * (1.0 / BAND) + 1e-6)
            re_out = (re * gain * quality).astype(BF16)
            im_out = (im * gain * quality).astype(BF16)
            im_cols = pl.multiple_of(part + cols, LANES)
            held[chunk][me, :, pl.ds(cols, LANES)] = re_out
            held[chunk][me, :, pl.ds(im_cols, LANES)] = im_out
            own[chunk, :, pl.ds(cols, LANES)] = re_out.astype(F32)
            own[chunk, :, pl.ds(im_cols, LANES)] = im_out.astype(F32)
            return carry

        lax.fori_loop(0, part // LANES, tile, 0)

    def line(chunk, step, way, block):
        slot = held[chunk].at[block * 2 + core]
        return pltpu.make_async_remote_copy(
            src_ref=slot, dst_ref=slot,
            send_sem=line_send.at[chunk, step, way], recv_sem=line_recv.at[chunk, step, way],
            device_id=(neighbour[way], my_hour), device_id_type=MESH)

    def to_twin(chunk, step, way, block, side):
        slot = held[chunk].at[block * 2 + side]
        return pltpu.make_async_remote_copy(
            src_ref=slot, dst_ref=slot,
            send_sem=twin_send.at[chunk, step, way], recv_sem=twin_recv.at[chunk, step, way],
            device_id=(twin, my_hour), device_id_type=MESH)

    def source(at, step, way):
        block = at - step if way == 0 else at + step
        beyond = range(at + 1, n_chip) if way == 0 else range(at)
        return block if 0 <= block < n_chip and any(to ^ block in apart for to in beyond) else None

    def any_chip(test):
        return functools.reduce(jnp.logical_or, [chip == at for at in range(n_chip) if test(at)], False)

    def sends(step, way):
        block = chip - step if way == 0 else chip + step
        return jnp.clip(block, 0, n_chip - 1), any_chip(lambda at: source(at, step, way) is not None)

    def before(at, step, way):
        giver = at - 1 if way == 0 else at + 1
        return source(giver, step, way) if 0 <= giver < n_chip else None

    def receives(step, way):
        block = chip - 1 - step if way == 0 else chip + 1 + step
        got = any_chip(lambda at: before(at, step, way) is not None)
        used = any_chip(lambda at: before(at, step, way) is not None and at ^ before(at, step, way) in apart)
        return jnp.clip(block, 0, n_chip - 1), got, used

    def run_if(ok, body):
        if ok is not False:
            pl.when(ok)(body)

    def start_line(chunk, step, way):
        block, ok = sends(step, way)
        run_if(ok, lambda: line(chunk, step, way, block).start())

    fetch.wait()
    whiten(0)
    pl.semaphore_wait(barrier, n_hour + (chip < n_chip - 1).astype(jnp.int32) + (chip > 0).astype(jnp.int32))

    for chunk in range(CHUNKS):
        if chunk:
            whiten(chunk)
        for way in range(2):
            start_line(chunk, 0, way)
        to_twin(chunk, 0, 0, chip, core).start()

    def pass_on(chunk, step):
        for way in range(2):
            block, got, used = receives(step, way)
            run_if(got, lambda: line(chunk, step, way, block).wait_recv())
            if step + 1 < n_chip - 1:
                start_line(chunk, step + 1, way)
            run_if(used, lambda: to_twin(chunk, step + 1, way, block, core).start())

    def work(chunk):
        to_twin(chunk, 0, 0, chip, 1 - core).wait_recv()
        for step in range(n_chip - 1):
            for way in range(2):
                block, _, used = receives(step, way)
                run_if(used, lambda: to_twin(chunk, step + 1, way, block, 1 - core).wait_recv())
        if chunk == 0:
            for load in loads:
                load.wait()
        for rnd in range(ROUNDS):
            partner = jnp.bitwise_xor(me, plan_ref[rnd])
            far[rnd] = held[chunk][partner].astype(F32)

        def tile(at, carry):
            rnd, cols = at // (part // LANES), at % (part // LANES) * LANES
            re_at = pl.ds(pl.multiple_of(cols, LANES), LANES)
            im_at = pl.ds(pl.multiple_of(part + cols, LANES), LANES)
            sums_re = [jnp.zeros((chans, LANES), F32)] * chans
            sums_im = [jnp.zeros((chans, LANES), F32)] * chans
            for hour in range(hours):
                own_re = own[chunk, hour * chans:(hour + 1) * chans, re_at]
                own_im = own[chunk, hour * chans:(hour + 1) * chans, im_at]
                for j in range(chans):
                    far_re = far[rnd, hour * chans + j:hour * chans + j + 1, re_at]
                    far_im = far[rnd, hour * chans + j:hour * chans + j + 1, im_at]
                    sums_re[j] += own_re * far_re + own_im * far_im
                    sums_im[j] += own_im * far_re - own_re * far_im
            for j in range(chans):
                start = (j // per_hour) * share + (rnd * per_hour + j % per_hour) * chans
                at_rows = pl.ds(pl.multiple_of(start, 8), chans)
                cross[at_rows, re_at] = sums_re[j]
                cross[at_rows, im_at] = sums_im[j]
            return carry

        lax.fori_loop(0, ROUNDS * (part // LANES), tile, 0)

        first, second = split(cross[...])
        lagged = jnp.dot(first, high[chunk], preferred_element_type=F32)
        lagged += jnp.dot(second, high[chunk], preferred_element_type=F32)
        lagged += jnp.dot(first, low[chunk], preferred_element_type=F32)
        if chunk == 0:
            total[...] = lagged
        else:
            total[...] += lagged

    for step in range(n_chip - 2):
        for chunk in range(CHUNKS):
            pass_on(chunk, step)
    for chunk in range(CHUNKS):
        pass_on(chunk, n_chip - 2)
        if chunk:
            work(chunk - 1)
    work(CHUNKS - 1)

    def give(step):
        goal = lax.rem(my_hour + step, n_hour)
        return pltpu.make_async_remote_copy(
            src_ref=rounded.at[pl.ds(pl.multiple_of(goal * share, 8), share)],
            dst_ref=arrived.at[step - 1],
            send_sem=sum_send.at[step - 1], recv_sem=sum_recv.at[step - 1],
            device_id=(me, goal), device_id_type=MESH)

    rounded[...] = total[...].astype(BF16)
    for step in range(1, n_hour):
        give(step).start()

    for chunk in range(CHUNKS):
        to_twin(chunk, 0, 0, chip, core).wait_send()
        for step in range(n_chip - 1):
            for way in range(2):
                block, ok = sends(step, way)
                run_if(ok, lambda: line(chunk, step, way, block).wait_send())
                block, _, used = receives(step, way)
                run_if(used, lambda: to_twin(chunk, step + 1, way, block, core).wait_send())

    result = total[pl.ds(pl.multiple_of(my_hour * share, 8), share), :]
    for step in range(1, n_hour):
        give(step).wait_recv()
        result += arrived[step - 1].astype(F32)
    out_ref[...] = result.reshape(ROUNDS, per_hour, chans, LAGS)
    for step in range(1, n_hour):
        give(step).wait_send()


def per_device(spectra, quality, plan):
    hours, chans, width = spectra.shape
    n_freq = width // 2
    n_chan, n_hour = lax.axis_size("chan"), lax.axis_size("hour")
    n_chip = n_chan // 2
    rows = hours * chans
    part = n_freq // CHUNKS
    per_hour = chans // n_hour
    share = ROUNDS * per_hour * chans
    high, low = lag_tables(n_freq, hours * n_hour, CHUNKS)
    smem, vmem, hbm = (pl.BlockSpec(memory_space=m) for m in (pltpu.SMEM, pltpu.VMEM, pltpu.HBM))
    dma = pltpu.SemaphoreType.DMA
    call = lambda index, apart: pl.pallas_call(
        functools.partial(kernel, (n_chan, n_hour, hours, chans, n_freq), apart),
        out_shape=jax.ShapeDtypeStruct((ROUNDS, per_hour, chans, LAGS), F32),
        in_specs=[smem, hbm, smem, hbm, hbm],
        out_specs=vmem,
        scratch_shapes=[pltpu.VMEM((n_chan, rows, 2 * part), BF16)] * CHUNKS + [
            pltpu.VMEM((CHUNKS, rows, 2 * part), F32),
            pltpu.VMEM((ROUNDS, rows, 2 * part), F32),
            pltpu.VMEM((n_hour * share, 2 * part), F32),
            pltpu.VMEM((n_hour * share, LAGS), F32),
            pltpu.VMEM((n_hour - 1, share, LAGS), BF16),
            pltpu.VMEM((n_hour * share, LAGS), BF16),
            pltpu.VMEM(spectra.shape, BF16),
            pltpu.VMEM(high.shape, BF16),
            pltpu.VMEM(low.shape, BF16),
            dma((3,)),
            dma((CHUNKS, n_chip - 1, 2)),
            dma((CHUNKS, n_chip - 1, 2)),
            dma((CHUNKS, n_chip, 2)),
            dma((CHUNKS, n_chip, 2)),
            dma((n_hour - 1,)),
            dma((n_hour - 1,)),
        ],
        compiler_params=pltpu.CompilerParams(
            collective_id=index, has_side_effects=True, vmem_limit_bytes=63 * 1024 * 1024 + 960 * 1024),
    )
    full = tuple(range(1, n_chip))
    kinds = [full, (1, 3), (2, 3)] if n_chip == 4 else [full]
    calls = [call(index, apart) for index, apart in enumerate(kinds)]
    operands = (plan, spectra, quality, jnp.asarray(high), jnp.asarray(low))
    if len(calls) == 1:
        return calls[0](*operands)
    by_one, by_two = (jnp.any(plan // 2 == offset) for offset in (1, 2))
    kind = jnp.where(by_one & ~by_two, 1, jnp.where(by_two & ~by_one, 2, 0))
    return lax.switch(kind, calls, *operands)


def solution(mesh):
    return jax.shard_map(
        per_device,
        mesh=mesh,
        in_specs=(P("hour", "chan", None), P("chan"), P()),
        out_specs=P(None, "hour", "chan", None),
        check_vma=False,
    )
```
